256 devices in a mesh: cyc: 16 (over y, x), row: 4 (over z_hi), col: 4 (over z_lo, core).
Axes of the slice: x: 4, y: 4, z: 8 (z_hi: 4, z_lo: 2; z = z_hi * 2 + z_lo), core: 2. Of those that a mesh axis runs over, the one named last changes fastest.
Arguments:
- raw: bfloat16 [32, 4, 1024, 2048], P('cyc', None, 'row', 'col'), may hold values from 0.099609375 to 4
- flat: float32 [4, 1024, 2048], P(None, 'row', 'col'), may hold values from 0.5 to 2
- dark: float32 [4, 1024, 2048], P(None, 'row', 'col'), may hold values from 0 to 1
- shifts: int32 [32, 8, 16, 2], P('cyc', 'row', 'col'), may hold values from -48 to 48, as said below
- fractions: int32 [32, 8, 16, 2], P('cyc', 'row', 'col'), may hold values from 0 to 7
Outputs:
- registered: bfloat16 [32, 4, 1024, 2048], P('cyc', None, 'row', 'col')
- scores: float32 [32, 32, 64], P('cyc', 'row', 'col')
The draws below stay inside these ranges and needn't reach their ends.
Inputs may be any that keep to these rules, and one draw needn't show every extreme that they name: `shifts`: each shift lies within 48 pixels; both ends are taken in every draw.
All inputs are finite; a program needn't handle non-finite values.
Results may differ from the reference program's by a relative error of at most 0.0041.
Values may be sent and summed in bfloat16 or wider, within the bound.
A program may use at most 128 MiB of HBM per device.

```python
import math
import jax
import jax.numpy as jnp
from jax import lax

CHANNELS = 4
TILE = 128
RADIUS = 4
SHIFT = 48
BOX = 32
CYCLES = 32
H = 1024
W = 2048
TROWS = 8
TCOLS = 16


def draw_shifts(key, part):
    key = jax.random.fold_in(key, 7)
    values = jax.random.randint(key, (CYCLES, H // TILE, W // TILE, 2), -SHIFT, SHIFT + 1, dtype=jnp.int32)
    values = values.at[0, 0, 0, 0].set(SHIFT)
    values = values.at[0, 0, 0, 1].set(-SHIFT)
    return values


def touch_ends(values, stream_key, least, top_value):
    spot = [jax.random.randint(jax.random.fold_in(stream_key, axis), (), 0, length) for axis, length in enumerate(values.shape)]
    widest = values.shape.index(max(values.shape))
    beside = spot[:widest] + [(spot[widest] + 1) % values.shape[widest]] + spot[widest + 1:]
    return values.at[tuple(spot)].set(least).at[tuple(beside)].set(top_value)


def levels(own_key, extent, cuts, smallest, high):
    level, own = 1.0, jax.random.fold_in(own_key, 6)
    for axis_at, blocks in cuts:
        draws = jnp.exp(jax.random.uniform(jax.random.fold_in(own, axis_at), (blocks,), jnp.float32, smallest / len(cuts), high / len(cuts)))
        level = level * jnp.repeat(draws, extent[axis_at] // blocks).reshape([-1 if axis == axis_at else 1 for axis in range(len(extent))])
    return level


def setup_inputs(seed: int = 0) -> dict:
    streams_of = jax.random.split(jax.random.key(seed), 6)
    return {
        "raw": jnp.clip(jnp.exp(math.log(4.0) - 3.6927934 * jax.random.uniform(streams_of[0], (CYCLES, CHANNELS, H, W), jnp.float32) ** levels(streams_of[0], (CYCLES, CHANNELS, H, W), ((0, 16), (2, 4), (3, 4)), -0.2, 0.2)), 0.099609375, 4.0).astype(jnp.bfloat16),
        "flat": jnp.clip(jnp.exp(math.log(2.0) - 1.3862944 * jax.random.uniform(streams_of[1], (CHANNELS, H, W), jnp.float32) ** levels(streams_of[1], (CHANNELS, H, W), ((1, 4), (2, 4)), -0.2, 0.2)), 0.5, 2.0),
        "dark": jnp.clip(1.0 * jax.random.uniform(streams_of[2], (CHANNELS, H, W), jnp.float32) ** levels(streams_of[2], (CHANNELS, H, W), ((1, 4), (2, 4)), -0.2, 0.2), 0.0, 1.0),
        "shifts": draw_shifts(jax.random.fold_in(streams_of[5], 71), 0),
        "fractions": touch_ends(jax.random.randint(streams_of[4], (CYCLES, TROWS, TCOLS, 2), 0, 8), jax.random.fold_in(streams_of[4], 1), 0, 7).astype(jnp.int32),
    }


def square_filter(image, start, combine):
    side = 2 * RADIUS + 1
    along_cols = lax.reduce_window(image, jnp.array(start, image.dtype), combine, (1, 1, side), (1, 1, 1), 'VALID')
    return lax.reduce_window(along_cols, jnp.array(start, image.dtype), combine, (1, side, 1), (1, 1, 1), 'VALID')

def top_hat(raw_cycle, dark, flat):
    corrected = (raw_cycle.astype(jnp.float32) - dark) / flat
    margin = 2 * RADIUS
    padded = jnp.pad(corrected, ((0, 0), (margin, margin), (margin, margin)))
    eroded = square_filter(padded, jnp.inf, lax.min)
    opened = square_filter(eroded, -jnp.inf, lax.max)
    return (corrected - opened).astype(jnp.bfloat16)

def one_tile(image, row_start, col_start, frac_row, frac_col):
    zero = jnp.zeros((), jnp.int32)
    block = lax.dynamic_slice(image, (zero, row_start, col_start), (image.shape[0], TILE + 1, TILE + 1)).astype(jnp.float32)
    lower = frac_row.astype(jnp.float32) / 8.0
    right = frac_col.astype(jnp.float32) / 8.0
    rows_mixed = block[:, :TILE, :] * (1.0 - lower) + block[:, 1:, :] * lower
    return rows_mixed[:, :, :TILE] * (1.0 - right) + rows_mixed[:, :, 1:] * right

def register(tophat, shift_cycle, frac_cycle):
    margin = SHIFT + 1
    padded = jnp.pad(tophat, ((0, 0), (margin, margin), (margin, margin)))
    tile_rows = shift_cycle.shape[0]
    tile_cols = shift_cycle.shape[1]
    base_rows = jnp.arange(tile_rows, dtype=jnp.int32)[:, None] * TILE + margin
    base_cols = jnp.arange(tile_cols, dtype=jnp.int32)[None, :] * TILE + margin
    row_start = (base_rows + shift_cycle[:, :, 0]).reshape(-1)
    col_start = (base_cols + shift_cycle[:, :, 1]).reshape(-1)
    tiles = jax.vmap(one_tile, in_axes=(None, 0, 0, 0, 0))(padded, row_start, col_start, frac_cycle[:, :, 0].reshape(-1), frac_cycle[:, :, 1].reshape(-1))
    tiles = tiles.reshape(tile_rows, tile_cols, tophat.shape[0], TILE, TILE)
    whole = tiles.transpose(2, 0, 3, 1, 4).reshape(tophat.shape)
    return whole.astype(jnp.bfloat16)

def box_scores(moving, fixed):
    lead = moving.shape[0]
    first = moving.astype(jnp.float32).reshape(lead, moving.shape[1] // BOX, BOX, moving.shape[2] // BOX, BOX)
    second = fixed.astype(jnp.float32).reshape(1, fixed.shape[0] // BOX, BOX, fixed.shape[1] // BOX, BOX)
    first = first - lax.optimization_barrier(jnp.mean(first, axis=(2, 4), keepdims=True))
    second = second - lax.optimization_barrier(jnp.mean(second, axis=(2, 4), keepdims=True))
    covar = lax.optimization_barrier(jnp.mean(first * second, axis=(2, 4)))
    var_first = lax.optimization_barrier(jnp.mean(first * first, axis=(2, 4)))
    var_second = lax.optimization_barrier(jnp.mean(second * second, axis=(2, 4)))
    return covar / jnp.sqrt(var_first * var_second + 1e-06)

def reference(raw, flat, dark, shifts, fractions):

    def per_cycle(items):
        raw_cycle, shift_cycle, frac_cycle = items
        return register(top_hat(raw_cycle, dark, flat), shift_cycle, frac_cycle)
    registered = lax.map(per_cycle, (raw, shifts, fractions))
    panel = registered[0, 0]
    scores = lax.map(lambda stain: box_scores(stain[None], panel)[0], registered[:, 0])
    return (registered, scores)
```

```python
import functools
import math

import jax
import jax.numpy as jnp
from jax import lax
from jax.experimental import pallas as pl
from jax.experimental.pallas import tpu as pltpu
from jax.sharding import PartitionSpec as P

TILE = 128
MARGIN = 8
ABOVE = 48
BELOW = 64
BOX = 32
LAG = 3
MESH = pl.DeviceIdType.MESH
F32 = jnp.float32
BF16 = jnp.bfloat16


def lane_iota(rows):
    return lax.broadcasted_iota(jnp.int32, (rows, TILE), 1)


def shifted(tiles, step):
    count = len(tiles)
    rolled = [pltpu.roll(tile, (-step) % TILE, 1) for tile in tiles]
    lane = lane_iota(tiles[0].shape[0])
    if step > 0:
        return [jnp.where(lane < TILE - step, rolled[t], rolled[(t + 1) % count]) for t in range(count)]
    return [jnp.where(lane >= -step, rolled[t], rolled[(t - 1) % count]) for t in range(count)]


def lane_window(tiles, combine, outputs):
    ahead, behind = shifted(tiles, 1), shifted(tiles, -1)
    three = [combine(combine(a, b), c) for a, b, c in zip(tiles, ahead, behind)]
    ahead, behind = shifted(three, 3), shifted(three, -3)
    return [combine(combine(three[t], ahead[t]), behind[t]) for t in range(outputs)]


def kernel(
    sizes, raw, flat, dark, shifts, fractions, out, scores,
    rawv, flatv, darkv, corr, pack_l, pack_r, halo_l, halo_r, tmp1, tmp2, hat, mixed, weights, reg, panel,
    sums, means,
    in_sem, out_sem, p_send, p_recv, c_send, c_recv, r_send, r_recv, h_send, h_recv, b_send, b_recv,
):
    n_cyc, n_row, n_col, nx = sizes
    ny = n_cyc // nx
    channels, rows, cols = flat.shape
    images = raw.shape[0] * channels
    lanes = cols // TILE
    cyc, row, col = lax.axis_index("cyc"), lax.axis_index("row"), lax.axis_index("col")
    yy, xx = cyc // nx, cyc % nx
    has_up, has_down = row > 0, row < n_row - 1
    has_left, has_right = col > 0, col < n_col - 1
    up, down = {"row": row - 1}, {"row": row + 1}
    left, right = {"col": col - 1}, {"col": col + 1}

    def in_copies(k):
        return (
            pltpu.make_async_copy(raw.at[:, k], rawv.at[:, k], in_sem.at[k, 0]),
            pltpu.make_async_copy(flat.at[k], flatv.at[k], in_sem.at[k, 1]),
            pltpu.make_async_copy(dark.at[k], darkv.at[k], in_sem.at[k, 2]),
        )

    for k in range(channels):
        for copy in in_copies(k):
            copy.start()

    barrier = pltpu.get_barrier_semaphore()

    def greet(device):
        pl.semaphore_signal(barrier, inc=1, device_id=device, device_id_type=MESH)

    for there, device in ((has_up, up), (has_down, down), (has_left, left), (has_right, right)):
        pl.when(there)(functools.partial(greet, device))
    for k in range(1, nx):
        pl.when(cyc == 0)(functools.partial(greet, {"cyc": k}))
    pl.when((yy == 0) & (xx > 0))(functools.partial(greet, {"cyc": 0}))
    for k in range(1, ny):
        pl.when(yy == 0)(functools.partial(greet, {"cyc": k * nx + xx}))
    pl.when(yy > 0)(functools.partial(greet, {"cyc": xx}))

    @pl.when(jnp.logical_not(has_up))
    def _():
        corr[:, :, 0:MARGIN, :] = jnp.zeros((images, lanes + 1, MARGIN, TILE), F32)
        hat[:, :, 0:ABOVE, :] = jnp.zeros((images, lanes + 2, ABOVE, TILE), BF16)

    @pl.when(jnp.logical_not(has_down))
    def _():
        corr[:, :, MARGIN + rows :, :] = jnp.zeros((images, lanes + 1, MARGIN, TILE), F32)
        hat[:, :, ABOVE + rows :, :] = jnp.zeros((images, lanes + 2, BELOW, TILE), BF16)

    @pl.when(jnp.logical_not(has_left))
    def _():
        halo_r[...] = jnp.zeros(halo_r.shape, F32)
        hat[:, 0, :, :] = jnp.zeros((images, ABOVE + rows + BELOW, TILE), BF16)

    @pl.when(jnp.logical_not(has_right))
    def _():
        halo_l[...] = jnp.zeros(halo_l.shape, F32)
        hat[:, lanes + 1, :, :] = jnp.zeros((images, ABOVE + rows + BELOW, TILE), BF16)

    def one(flag):
        return jnp.where(flag, 1, 0)

    expected = one(has_up) + one(has_down) + one(has_left) + one(has_right)
    expected += jnp.where(yy == 0, jnp.where(xx == 0, nx - 1, 1) + ny - 1, 1)
    pl.semaphore_wait(barrier, expected)

    def remote(source, target, send, recv, device):
        return pltpu.make_async_remote_copy(
            src_ref=source, dst_ref=target, send_sem=send, recv_sem=recv, device_id=device, device_id_type=MESH
        )

    def edge_rows(i):
        blocks = pl.ds(0, lanes)
        return (
            (has_down, has_up, remote(
                corr.at[i, blocks, pl.ds(rows, MARGIN)], corr.at[i, blocks, pl.ds(0, MARGIN)],
                p_send.at[i, 0], p_recv.at[i, 0], down)),
            (has_up, has_down, remote(
                corr.at[i, blocks, pl.ds(MARGIN, MARGIN)], corr.at[i, blocks, pl.ds(MARGIN + rows, MARGIN)],
                p_send.at[i, 1], p_recv.at[i, 1], up)),
        )

    def start(moves):
        for sends, _, copy in moves:
            pl.when(sends)(copy.start)

    def received(moves):
        for _, receives, copy in moves:
            pl.when(receives)(copy.wait_recv)

    def sent(moves):
        for sends, _, copy in moves:
            pl.when(sends)(copy.wait_send)

    def correct(k, carry):
        for copy in in_copies(k):
            copy.wait()

        def block(b, carry):
            at = pl.ds(pl.multiple_of(b * 16, 16), 16)
            to = pl.ds(pl.multiple_of(b * 16 + MARGIN, 8), 16)
            gain = 1.0 / flatv[k, at, :]
            offset = darkv[k, at, :]
            for c in range(images // channels):
                value = (rawv[c, k, at, :].astype(F32) - offset) * gain
                for t in range(lanes):
                    corr[c * channels + k, t, to, :] = value[:, t * TILE : (t + 1) * TILE]
            return carry

        lax.fori_loop(0, rows // 16, block, 0)
        for c in range(images // channels):
            start(edge_rows(c * channels + k))
        return carry

    lax.fori_loop(0, channels, correct, 0)

    tile_rows, tile_cols = rows // TILE, cols // TILE
    tiles = tile_rows * tile_cols
    source = lax.broadcasted_iota(jnp.int32, (3 * TILE, TILE), 0)
    target = lax.broadcasted_iota(jnp.int32, (3 * TILE, TILE), 1)
    apart = (source - target).astype(F32)

    def weigh(n, carry):
        c, rest = n // tiles, n % tiles
        i, j = rest // tile_cols, rest % tile_cols
        place = (shifts[c, i, j, 1] + TILE).astype(F32) + fractions[c, i, j, 1].astype(F32) / 8.0
        weights[n] = jnp.maximum(1.0 - jnp.abs(apart - place), 0.0).astype(BF16)
        return carry

    lax.fori_loop(0, (images // channels) * tiles, weigh, 0)

    def arrived(i, carry):
        received(edge_rows(i))
        return carry

    lax.fori_loop(0, images, arrived, 0)
    high = rows + 2 * MARGIN

    def pack(b, carry):
        at = pl.ds(pl.multiple_of(b * 8, 8), 8)
        lane = lane_iota(8)
        first = jnp.zeros((8, TILE), F32)
        last = jnp.zeros((8, TILE), F32)
        for i in range(images):
            low = pltpu.roll(corr[i, 0, at, :], MARGIN * i, 1)
            first = jnp.where((lane >= MARGIN * i) & (lane < MARGIN * (i + 1)), low, first)
            top = pltpu.roll(corr[i, lanes - 1, at, :], (72 + MARGIN * i) % TILE, 1)
            spot = 64 + MARGIN * i
            last = jnp.where((lane >= spot) & (lane < spot + MARGIN), top, last)
        pack_l[at, :] = first
        pack_r[at, :] = last
        return carry

    lax.fori_loop(0, high // 8, pack, 0)
    edge_cols = (
        (has_left, has_right, remote(pack_l, halo_l, c_send.at[0], c_recv.at[0], left)),
        (has_right, has_left, remote(pack_r, halo_r, c_send.at[1], c_recv.at[1], right)),
    )
    start(edge_cols)
    received(edge_cols)

    lo = MARGIN

    def hat_rows(i):
        blocks = pl.ds(1, lanes)
        return (
            (has_down, has_up, remote(
                hat.at[i, blocks, pl.ds(rows, ABOVE)], hat.at[i, blocks, pl.ds(0, ABOVE)],
                r_send.at[i, 0], r_recv.at[i, 0], down)),
            (has_up, has_down, remote(
                hat.at[i, blocks, pl.ds(ABOVE, BELOW)], hat.at[i, blocks, pl.ds(ABOVE + rows, BELOW)],
                r_send.at[i, 1], r_recv.at[i, 1], up)),
        )

    def hat_cols(i, part):
        at = pl.ds((ABOVE, 0, ABOVE + rows)[part], (rows, ABOVE, BELOW)[part])
        return (
            (has_left, has_right, remote(
                hat.at[i, 1, at], hat.at[i, lanes + 1, at], h_send.at[i, part, 0], h_recv.at[i, part, 0], left)),
            (has_right, has_left, remote(
                hat.at[i, lanes, at], hat.at[i, 0, at], h_send.at[i, part, 1], h_recv.at[i, part, 1], right)),
        )

    def tophat(i):
        turn_l = lax.rem(TILE - MARGIN * i, TILE)
        turn_r = 56 - MARGIN * i

        def erode_cols(b, carry):
            at = pl.ds(pl.multiple_of(b * 16, 16), 16)
            to = pl.ds(pl.multiple_of(b * 16 + lo, 8), 16)
            sides = jnp.where(
                lane_iota(16) < 64, pltpu.roll(halo_l[at, :], turn_l, 1), pltpu.roll(halo_r[at, :], turn_r, 1)
            )
            now = [corr[i, t, at, :] for t in range(lanes)] + [sides]
            for t, value in enumerate(lane_window(now, jnp.minimum, lanes + 1)):
                tmp1[t, to, :] = value
            return carry

        lax.fori_loop(0, high // 16, erode_cols, 0)

        def row_three(combine, count):
            def block(b, carry):
                base = b * 16 + lo
                for t in range(count):
                    value = combine(
                        combine(tmp1[t, pl.ds(base - 1, 16), :], tmp1[t, pl.ds(base, 16), :]),
                        tmp1[t, pl.ds(base + 1, 16), :],
                    )
                    tmp2[t, pl.ds(base, 16), :] = value
                return carry

            lax.fori_loop(0, high // 16, block, 0)

        def row_nine(combine, t, base):
            return combine(
                combine(tmp2[t, pl.ds(base - 3, 16), :], tmp2[t, pl.ds(base, 16), :]), tmp2[t, pl.ds(base + 3, 16), :]
            )

        row_three(jnp.minimum, lanes + 1)

        def erode_rows(b, carry):
            base = b * 16 + lo
            now = [row_nine(jnp.minimum, t, base) for t in range(lanes + 1)]
            for t, value in enumerate(lane_window(now, jnp.maximum, lanes)):
                tmp1[t, pl.ds(base, 16), :] = value
            return carry

        lax.fori_loop(0, high // 16, erode_rows, 0)
        row_three(jnp.maximum, lanes)

        def subtract(b, carry):
            base = b * 16 + MARGIN
            to = pl.ds(pl.multiple_of(b * 16 + ABOVE, 16), 16)
            for t in range(lanes):
                value = corr[i, t, pl.ds(base, 16), :] - row_nine(jnp.maximum, t, base + lo)
                hat[i, t + 1, to, :] = value.astype(BF16)
            return carry

        lax.fori_loop(0, rows // 16, subtract, 0)
        start(hat_rows(i))
        start(hat_cols(i, 0))

    def corners(i):
        received(hat_rows(i))
        for part in (1, 2):
            start(hat_cols(i, part))

    def out_copy(i):
        return pltpu.make_async_copy(reg.at[i], out.at[i // channels, i % channels], out_sem.at[i])

    def resample(i):
        for part in range(3):
            received(hat_cols(i, part))
        c = i // channels
        span = TILE + ABOVE + BELOW
        for n in range(tiles):
            ti, tj = n // tile_cols, n % tile_cols
            window = pl.ds(ti * TILE, span)
            near = jnp.concatenate([hat[i, tj + t, window, :] for t in range(3)], axis=1)
            moved = jnp.dot(near, weights[c * tiles + n], preferred_element_type=F32)
            mixed[n] = pltpu.roll(moved, (span - ABOVE) - shifts[c, ti, tj, 0], 0)
            lower = fractions[c, ti, tj, 0].astype(F32) / 8.0
            value = mixed[n, 0:TILE, :] * (1.0 - lower) + mixed[n, 1 : TILE + 1, :] * lower
            reg[i, ti * TILE : (ti + 1) * TILE, tj * TILE : (tj + 1) * TILE] = value.astype(BF16)
        out_copy(i).start()

    def panel_copy(device, slot):
        return remote(panel, panel, b_send.at[slot], b_recv.at[0], {"cyc": device})

    def ordered(j):
        return lax.rem(j, 2) * channels + lax.div(j, 2)

    def to_columns(act):
        for k in range(1, ny):
            act(panel_copy(k * nx + xx, nx + k))

    def to_row(act):
        for k in range(1, nx):
            act(panel_copy(k, k))

    def begin(copy):
        copy.start()

    def end(copy):
        copy.wait_send()

    def step(s, carry):
        @pl.when(s < images)
        def _():
            tophat(ordered(s))

        @pl.when((s >= LAG) & (s < LAG + images))
        def _():
            corners(ordered(s - LAG))

        @pl.when(s >= LAG + 1)
        def _():
            resample(ordered(s - LAG - 1))

        @pl.when((s == LAG + 1) & (cyc == 0))
        def _():
            panel[...] = reg[0]
            to_row(begin)
            to_columns(begin)

        @pl.when((s == LAG + 5) & (yy == 0) & (xx > 0))
        def _():
            panel_copy(0, 0).wait_recv()
            to_columns(begin)

        return carry

    lax.fori_loop(0, images + LAG + 1, step, 0)

    @pl.when(yy > 0)
    def _():
        panel_copy(0, 0).wait_recv()

    box_rows, box_cols = rows // BOX, cols // BOX
    gather = (lax.broadcasted_iota(jnp.int32, (cols, box_cols), 0) // BOX
              == lax.broadcasted_iota(jnp.int32, (cols, box_cols), 1)).astype(F32)
    spread = (lax.broadcasted_iota(jnp.int32, (box_cols, cols), 1) // BOX
              == lax.broadcasted_iota(jnp.int32, (box_cols, cols), 0)).astype(F32)
    exact = functools.partial(jnp.dot, precision=lax.Precision.HIGHEST, preferred_element_type=F32)
    area = 1.0 / (BOX * BOX)

    def stains(b):
        at = pl.ds(b * BOX, BOX)
        return [reg[c * channels, at, :].astype(F32) for c in range(images // channels)] + [panel[at, :].astype(F32)]

    for b in range(box_rows):
        for n, value in enumerate(stains(b)):
            sums[n, pl.ds(b, 1), :] = jnp.sum(value, axis=0, keepdims=True)
    cycles = images // channels
    for n in range(cycles + 1):
        means[n] = exact(exact(sums[n], gather) * area, spread)
    for b in range(box_rows):
        centred = [value - means[n, pl.ds(b, 1), :] for n, value in enumerate(stains(b))]
        fixed = centred[cycles]
        terms = [value * fixed for value in centred] + [value * value for value in centred[:cycles]]
        for n, value in enumerate(terms):
            sums[n, pl.ds(b, 1), :] = jnp.sum(value, axis=0, keepdims=True)
    fixed_var = exact(sums[cycles], gather) * area
    for c in range(cycles):
        covar = exact(sums[c], gather) * area
        var = exact(sums[cycles + 1 + c], gather) * area
        scores[c] = covar / jnp.sqrt(var * fixed_var + 1e-06)

    def finish(i, carry):
        sent(edge_rows(i))
        sent(hat_rows(i))
        for part in range(3):
            sent(hat_cols(i, part))
        out_copy(i).wait()
        return carry

    lax.fori_loop(0, images, finish, 0)
    sent(edge_cols)

    @pl.when(cyc == 0)
    def _():
        to_row(end)

    @pl.when(yy == 0)
    def _():
        to_columns(end)


def body(sizes, raw, flat, dark, shifts, fractions):
    cycles, channels, rows, cols = raw.shape
    images, lanes = cycles * channels, cols // TILE
    tiles = (rows // TILE) * lanes
    high = rows + 2 * MARGIN
    dma = pltpu.SemaphoreType.DMA
    anywhere = pl.BlockSpec(memory_space=pl.ANY)
    scalars = pl.BlockSpec(memory_space=pltpu.SMEM)
    vmem = pl.BlockSpec(memory_space=pltpu.VMEM)
    nx = math.isqrt(sizes[0])
    registered, scores = pl.pallas_call(
        functools.partial(kernel, sizes + (nx,)),
        out_shape=(
            jax.ShapeDtypeStruct(raw.shape, BF16),
            jax.ShapeDtypeStruct((cycles, rows // BOX, cols // BOX), F32),
        ),
        in_specs=[anywhere, anywhere, anywhere, scalars, scalars],
        out_specs=(anywhere, vmem),
        scratch_shapes=[
            pltpu.VMEM(raw.shape, BF16),
            pltpu.VMEM(flat.shape, F32),
            pltpu.VMEM(dark.shape, F32),
            pltpu.VMEM((images, lanes + 1, high, TILE), F32),
            pltpu.VMEM((high, TILE), F32),
            pltpu.VMEM((high, TILE), F32),
            pltpu.VMEM((high, TILE), F32),
            pltpu.VMEM((high, TILE), F32),
            pltpu.VMEM((lanes + 1, high + 2 * MARGIN, TILE), F32),
            pltpu.VMEM((lanes + 1, high + 2 * MARGIN, TILE), F32),
            pltpu.VMEM((images, lanes + 2, ABOVE + rows + BELOW, TILE), BF16),
            pltpu.VMEM((tiles, TILE + ABOVE + BELOW, TILE), F32),
            pltpu.VMEM((cycles * tiles, 3 * TILE, TILE), BF16),
            pltpu.VMEM((images, rows, cols), BF16),
            pltpu.VMEM((rows, cols), BF16),
            pltpu.VMEM((2 * cycles + 1, rows // BOX, cols), F32),
            pltpu.VMEM((cycles + 1, rows // BOX, cols), F32),
            dma((channels, 3)),
            dma((images,)),
            dma((images, 2)),
            dma((images, 2)),
            dma((2,)),
            dma((2,)),
            dma((images, 2)),
            dma((images, 2)),
            dma((images, 3, 2)),
            dma((images, 3, 2)),
            dma((nx + sizes[0] // nx,)),
            dma((1,)),
        ],
        compiler_params=pltpu.CompilerParams(
            collective_id=0, has_side_effects=True, vmem_limit_bytes=56 * 1024 * 1024
        ),
    )(raw, flat, dark, shifts, fractions)
    return registered, scores


def solution(mesh):
    sizes = (mesh.shape["cyc"], mesh.shape["row"], mesh.shape["col"])
    return jax.shard_map(
        functools.partial(body, sizes),
        mesh=mesh,
        in_specs=(
            P("cyc", None, "row", "col"),
            P(None, "row", "col"),
            P(None, "row", "col"),
            P("cyc", "row", "col", None),
            P("cyc", "row", "col", None),
        ),
        out_specs=(P("cyc", None, "row", "col"), P("cyc", "row", "col")),
        check_vma=False,
    )
```

```python
import functools
import math

import jax
import jax.numpy as jnp
from jax import lax
from jax.experimental import pallas as pl
from jax.experimental.pallas import tpu as pltpu
from jax.sharding import PartitionSpec as P

TILE = 128
MARGIN = 8
ABOVE = 48
BELOW = 64
EDGE = 16
CHUNK = 136
BOX = 32
LAG = 3
MESH = pl.DeviceIdType.MESH
F32 = jnp.float32
BF16 = jnp.bfloat16


def spread_three(source, target, combine, start, count):
    for at in range(start, start + count, CHUNK):
        size = min(CHUNK, start + count - at)
        near = combine(source[pl.ds(at - 1, size), :], source[pl.ds(at, size), :])
        target[pl.ds(at, size), :] = combine(near, source[pl.ds(at + 1, size), :])


def spread_nine(source, combine, at, size):
    near = combine(source[pl.ds(at - 3, size), :], source[pl.ds(at, size), :])
    return combine(near, source[pl.ds(at + 3, size), :])


def kernel(
    sizes, raw, flat, dark, shifts, fractions, out, scores,
    rawv, flatv, darkv, corr, tall, brims, brims_back, wide1, wide2, three, back, hat, next_s, next_r, mixed, weights, reg, panel,
    sums, means,
    in_sem, out_sem, p_send, p_recv, c_send, c_recv, r_send, r_recv, n_send, n_recv, h_send, h_recv, b_send, b_recv,
):
    n_cyc, n_row, n_col, nx = sizes
    ny = n_cyc // nx
    channels, rows, cols = flat.shape
    images = raw.shape[0] * channels
    lanes = cols // TILE
    cyc, row, col = lax.axis_index("cyc"), lax.axis_index("row"), lax.axis_index("col")
    yy, xx = cyc // nx, cyc % nx
    has_up, has_down = row > 0, row < n_row - 1
    has_left, has_right = col > 0, col < n_col - 1
    up, down = {"row": row - 1}, {"row": row + 1}
    left, right = {"col": col - 1}, {"col": col + 1}

    def in_copies(k):
        return (
            pltpu.make_async_copy(raw.at[:, k], rawv.at[:, k], in_sem.at[k, 0]),
            pltpu.make_async_copy(flat.at[k], flatv.at[k], in_sem.at[k, 1]),
            pltpu.make_async_copy(dark.at[k], darkv.at[k], in_sem.at[k, 2]),
        )

    for k in range(channels):
        for copy in in_copies(k):
            copy.start()

    barrier = pltpu.get_barrier_semaphore()

    def greet(device):
        pl.semaphore_signal(barrier, inc=1, device_id=device, device_id_type=MESH)

    for there, device in ((has_up, up), (has_down, down), (has_left, left), (has_right, right)):
        pl.when(there)(functools.partial(greet, device))
    for k in range(1, nx):
        pl.when(cyc == 0)(functools.partial(greet, {"cyc": k}))
    pl.when((yy == 0) & (xx > 0))(functools.partial(greet, {"cyc": 0}))
    for k in range(1, ny):
        pl.when(yy == 0)(functools.partial(greet, {"cyc": k * nx + xx}))
    pl.when(yy > 0)(functools.partial(greet, {"cyc": xx}))

    next_s[...] = jnp.zeros(next_s.shape, F32)

    @pl.when(jnp.logical_not(has_up))
    def _():
        corr[:, :, MARGIN:EDGE, :] = jnp.zeros((images, lanes, MARGIN, TILE), F32)
        hat[:, :, 0:ABOVE, :] = jnp.zeros((images, lanes + 2, ABOVE, TILE), BF16)

    @pl.when(jnp.logical_not(has_down))
    def _():
        corr[:, :, EDGE + rows : EDGE + rows + MARGIN, :] = jnp.zeros((images, lanes, MARGIN, TILE), F32)
        hat[:, :, ABOVE + rows :, :] = jnp.zeros((images, lanes + 2, BELOW, TILE), BF16)

    @pl.when(jnp.logical_not(has_left))
    def _():
        tall[:, MARGIN:EDGE, :] = jnp.zeros((2 * images + 1, MARGIN, TILE), F32)
        hat[:, 0, :, :] = jnp.zeros((images, ABOVE + rows + BELOW, TILE), BF16)

    @pl.when(jnp.logical_not(has_right))
    def _():
        tall[:, EDGE + cols : EDGE + cols + MARGIN, :] = jnp.zeros((2 * images + 1, MARGIN, TILE), F32)
        hat[:, lanes + 1, :, :] = jnp.zeros((images, ABOVE + rows + BELOW, TILE), BF16)

    def one(flag):
        return jnp.where(flag, 1, 0)

    expected = one(has_up) + one(has_down) + one(has_left) + one(has_right)
    expected += jnp.where(yy == 0, jnp.where(xx == 0, nx - 1, 1) + ny - 1, 1)
    pl.semaphore_wait(barrier, expected)

    def remote(source, target, send, recv, device):
        return pltpu.make_async_remote_copy(
            src_ref=source, dst_ref=target, send_sem=send, recv_sem=recv, device_id=device, device_id_type=MESH
        )

    def edge_rows(i):
        return (
            (has_down, has_up, remote(
                corr.at[i, :, pl.ds(rows + MARGIN, MARGIN)], corr.at[i, :, pl.ds(MARGIN, MARGIN)],
                p_send.at[i, 0], p_recv.at[i, 0], down)),
            (has_up, has_down, remote(
                corr.at[i, :, pl.ds(EDGE, MARGIN)], corr.at[i, :, pl.ds(EDGE + rows, MARGIN)],
                p_send.at[i, 1], p_recv.at[i, 1], up)),
        )

    def start(moves):
        for sends, _, copy in moves:
            pl.when(sends)(copy.start)

    def received(moves):
        for _, receives, copy in moves:
            pl.when(receives)(copy.wait_recv)

    def sent(moves):
        for sends, _, copy in moves:
            pl.when(sends)(copy.wait_send)

    def correct(k, carry):
        for copy in in_copies(k):
            copy.wait()

        def block(b, carry):
            at = pl.ds(pl.multiple_of(b * 16, 16), 16)
            to = pl.ds(pl.multiple_of(b * 16 + EDGE, 16), 16)
            gain = 1.0 / flatv[k, at, :]
            offset = darkv[k, at, :]
            for c in range(images // channels):
                value = (rawv[c, k, at, :].astype(F32) - offset) * gain
                for t in range(lanes):
                    corr[c * channels + k, t, to, :] = value[:, t * TILE : (t + 1) * TILE]
            return carry

        lax.fori_loop(0, rows // 16, block, 0)
        for c in range(images // channels):
            start(edge_rows(c * channels + k))
        return carry

    lax.fori_loop(0, channels, correct, 0)

    tile_rows, tile_cols = rows // TILE, cols // TILE
    tiles = tile_rows * tile_cols
    source = lax.broadcasted_iota(jnp.int32, (3 * TILE, TILE), 0)
    target = lax.broadcasted_iota(jnp.int32, (3 * TILE, TILE), 1)
    apart = (source - target).astype(F32)

    def weigh(n, carry):
        c, rest = n // tiles, n % tiles
        i, j = rest // tile_cols, rest % tile_cols
        place = (shifts[c, i, j, 1] + TILE).astype(F32) + fractions[c, i, j, 1].astype(F32) / 8.0
        weights[n] = jnp.maximum(1.0 - jnp.abs(apart - place), 0.0).astype(BF16)
        return carry

    lax.fori_loop(0, (images // channels) * tiles, weigh, 0)

    halves = rows // TILE
    brims[:, images * MARGIN :, :] = jnp.zeros((lanes, TILE - images * MARGIN, TILE), F32)
    upper = lax.broadcasted_iota(jnp.int32, (MARGIN, TILE), 0) >= MARGIN // 2

    def erode(i, carry):
        received(edge_rows(i))
        for t in range(lanes):
            spread_three(corr.at[i, t], three.at[t], jnp.minimum, MARGIN, rows + 2 * MARGIN)
        for t in range(lanes):
            for b in range(halves):
                value = spread_nine(three.at[t], jnp.minimum, EDGE + b * TILE, TILE)
                tall[halves * i + b, EDGE + t * TILE : EDGE + (t + 1) * TILE, :] = value.T
            above = spread_nine(three.at[t], jnp.minimum, MARGIN, MARGIN)
            below = spread_nine(three.at[t], jnp.minimum, EDGE + rows, MARGIN)
            brims[t, pl.ds(pl.multiple_of(MARGIN * i, MARGIN), MARGIN), :] = jnp.where(upper, above, below)
        return carry

    lax.fori_loop(0, images, erode, 0)
    for t in range(lanes):
        tall[halves * images, EDGE + t * TILE : EDGE + (t + 1) * TILE, :] = brims[t].T
    edge_cols = (
        (has_left, has_right, remote(
            tall.at[:, pl.ds(EDGE, MARGIN)], tall.at[:, pl.ds(EDGE + cols, MARGIN)],
            c_send.at[0], c_recv.at[0], left)),
        (has_right, has_left, remote(
            tall.at[:, pl.ds(cols + MARGIN, MARGIN)], tall.at[:, pl.ds(MARGIN, MARGIN)],
            c_send.at[1], c_recv.at[1], right)),
    )
    start(edge_cols)
    received(edge_cols)

    def across(n, place):
        spread_three(tall.at[n], wide1, jnp.minimum, MARGIN, cols + 2 * MARGIN)
        for at in range(MARGIN, cols + EDGE + MARGIN, CHUNK):
            size = min(CHUNK, cols + EDGE + MARGIN - at)
            wide2[at : at + size, :] = spread_nine(wide1, jnp.minimum, at, size)
        spread_three(wide2, wide1, jnp.maximum, MARGIN, cols + 2 * MARGIN)
        for t in range(lanes):
            place(t, spread_nine(wide1, jnp.maximum, EDGE + t * TILE, TILE).T)

    def keep_brims(t, value):
        brims_back[t] = value

    across(halves * images, keep_brims)

    def hat_rows(i):
        blocks = pl.ds(1, lanes)
        return (
            (has_down, has_up, remote(
                hat.at[i, blocks, pl.ds(rows, ABOVE)], hat.at[i, blocks, pl.ds(0, ABOVE)],
                r_send.at[i, 0], r_recv.at[i, 0], down)),
            (has_up, has_down, remote(
                hat.at[i, blocks, pl.ds(ABOVE, ABOVE)], hat.at[i, blocks, pl.ds(ABOVE + rows, ABOVE)],
                r_send.at[i, 1], r_recv.at[i, 1], up)),
            (has_up, has_down, remote(next_s.at[i], next_r.at[i], n_send.at[i], n_recv.at[i], up)),
        )

    def hat_cols(i, part):
        at = pl.ds((ABOVE, 0, ABOVE + rows)[part], (rows, ABOVE, BELOW)[part])
        return (
            (has_left, has_right, remote(
                hat.at[i, 1, at], hat.at[i, lanes + 1, at], h_send.at[i, part, 0], h_recv.at[i, part, 0], left)),
            (has_right, has_left, remote(
                hat.at[i, lanes, at], hat.at[i, 0, at], h_send.at[i, part, 1], h_recv.at[i, part, 1], right)),
        )

    def tophat(i):
        for b in range(halves):
            def keep(t, value, b=b):
                back[t, EDGE + b * TILE : EDGE + (b + 1) * TILE, :] = value

            across(halves * i + b, keep)
        for t in range(lanes):
            ends = brims_back[t, pl.ds(pl.multiple_of(MARGIN * i, MARGIN), MARGIN), :]
            back[t, MARGIN:EDGE, :] = ends
            back[t, EDGE + rows : EDGE + rows + MARGIN, :] = ends
        for t in range(lanes):
            spread_three(back.at[t], three.at[t], jnp.maximum, MARGIN, rows + 2 * MARGIN)
        for t in range(lanes):
            for b in range(halves):
                opened = spread_nine(three.at[t], jnp.maximum, EDGE + b * TILE, TILE)
                value = (corr[i, t, EDGE + b * TILE : EDGE + (b + 1) * TILE, :] - opened).astype(BF16)
                hat[i, t + 1, ABOVE + b * TILE : ABOVE + (b + 1) * TILE, :] = value
                if b == 0:
                    next_s[i, t : t + 1, :] = value[ABOVE : ABOVE + 16].astype(F32)[0:1]
        start(hat_rows(i))
        start(hat_cols(i, 0))

    def corners(i):
        received(hat_rows(i))

        @pl.when(has_down)
        def _():
            first = lax.broadcasted_iota(jnp.int32, (16, TILE), 0) == 0
            for t in range(lanes):
                value = jnp.where(first, next_r[i, t : t + 1, :], 0.0)
                hat[i, t + 1, ABOVE + rows + ABOVE :, :] = value.astype(BF16)

        for part in (1, 2):
            start(hat_cols(i, part))

    def out_copy(i):
        return pltpu.make_async_copy(reg.at[i], out.at[i // channels, i % channels], out_sem.at[i])

    def resample(i):
        for part in range(3):
            received(hat_cols(i, part))
        c = i // channels
        span = TILE + ABOVE + BELOW
        for n in range(tiles):
            ti, tj = n // tile_cols, n % tile_cols
            window = pl.ds(ti * TILE, span)
            near = jnp.concatenate([hat[i, tj + t, window, :] for t in range(3)], axis=1)
            moved = jnp.dot(near, weights[c * tiles + n], preferred_element_type=F32)
            mixed[n] = pltpu.roll(moved, (span - ABOVE) - shifts[c, ti, tj, 0], 0)
            lower = fractions[c, ti, tj, 0].astype(F32) / 8.0
            value = mixed[n, 0:TILE, :] * (1.0 - lower) + mixed[n, 1 : TILE + 1, :] * lower
            reg[i, ti * TILE : (ti + 1) * TILE, tj * TILE : (tj + 1) * TILE] = value.astype(BF16)
        out_copy(i).start()

    def panel_copy(device, slot):
        return remote(panel, panel, b_send.at[slot], b_recv.at[0], {"cyc": device})

    def ordered(j):
        return lax.rem(j, 2) * channels + lax.div(j, 2)

    def to_columns(act):
        for k in range(1, ny):
            act(panel_copy(k * nx + xx, nx + k))

    def to_row(act):
        for k in range(1, nx):
            act(panel_copy(k, k))

    def begin(copy):
        copy.start()

    def end(copy):
        copy.wait_send()

    def step(s, carry):
        @pl.when(s < images)
        def _():
            tophat(ordered(s))

        @pl.when((s >= LAG) & (s < LAG + images))
        def _():
            corners(ordered(s - LAG))

        @pl.when(s >= LAG + 1)
        def _():
            resample(ordered(s - LAG - 1))

        @pl.when((s == LAG + 1) & (cyc == 0))
        def _():
            panel[...] = reg[0]
            to_row(begin)
            to_columns(begin)

        @pl.when((s == LAG + 5) & (yy == 0) & (xx > 0))
        def _():
            panel_copy(0, 0).wait_recv()
            to_columns(begin)

        return carry

    lax.fori_loop(0, images + LAG + 1, step, 0)

    @pl.when(yy > 0)
    def _():
        panel_copy(0, 0).wait_recv()

    box_rows, box_cols = rows // BOX, cols // BOX
    gather = (lax.broadcasted_iota(jnp.int32, (cols, box_cols), 0) // BOX
              == lax.broadcasted_iota(jnp.int32, (cols, box_cols), 1)).astype(F32)
    spread = (lax.broadcasted_iota(jnp.int32, (box_cols, cols), 1) // BOX
              == lax.broadcasted_iota(jnp.int32, (box_cols, cols), 0)).astype(F32)
    exact = functools.partial(jnp.dot, precision=lax.Precision.HIGHEST, preferred_element_type=F32)
    area = 1.0 / (BOX * BOX)

    def stains(b):
        at = pl.ds(b * BOX, BOX)
        return [reg[c * channels, at, :].astype(F32) for c in range(images // channels)] + [panel[at, :].astype(F32)]

    for b in range(box_rows):
        for n, value in enumerate(stains(b)):
            sums[n, pl.ds(b, 1), :] = jnp.sum(value, axis=0, keepdims=True)
    cycles = images // channels
    for n in range(cycles + 1):
        means[n] = exact(exact(sums[n], gather) * area, spread)
    for b in range(box_rows):
        centred = [value - means[n, pl.ds(b, 1), :] for n, value in enumerate(stains(b))]
        fixed = centred[cycles]
        terms = [value * fixed for value in centred] + [value * value for value in centred[:cycles]]
        for n, value in enumerate(terms):
            sums[n, pl.ds(b, 1), :] = jnp.sum(value, axis=0, keepdims=True)
    fixed_var = exact(sums[cycles], gather) * area
    for c in range(cycles):
        covar = exact(sums[c], gather) * area
        var = exact(sums[cycles + 1 + c], gather) * area
        scores[c] = covar / jnp.sqrt(var * fixed_var + 1e-06)

    def finish(i, carry):
        sent(edge_rows(i))
        sent(hat_rows(i))
        for part in range(3):
            sent(hat_cols(i, part))
        out_copy(i).wait()
        return carry

    lax.fori_loop(0, images, finish, 0)
    sent(edge_cols)

    @pl.when(cyc == 0)
    def _():
        to_row(end)

    @pl.when(yy == 0)
    def _():
        to_columns(end)


def body(sizes, raw, flat, dark, shifts, fractions):
    cycles, channels, rows, cols = raw.shape
    images, lanes = cycles * channels, cols // TILE
    tiles = (rows // TILE) * lanes
    dma = pltpu.SemaphoreType.DMA
    anywhere = pl.BlockSpec(memory_space=pl.ANY)
    scalars = pl.BlockSpec(memory_space=pltpu.SMEM)
    vmem = pl.BlockSpec(memory_space=pltpu.VMEM)
    nx = math.isqrt(sizes[0])
    registered, scores = pl.pallas_call(
        functools.partial(kernel, sizes + (nx,)),
        out_shape=(
            jax.ShapeDtypeStruct(raw.shape, BF16),
            jax.ShapeDtypeStruct((cycles, rows // BOX, cols // BOX), F32),
        ),
        in_specs=[anywhere, anywhere, anywhere, scalars, scalars],
        out_specs=(anywhere, vmem),
        scratch_shapes=[
            pltpu.VMEM(raw.shape, BF16),
            pltpu.VMEM(flat.shape, F32),
            pltpu.VMEM(dark.shape, F32),
            pltpu.VMEM((images, lanes, rows + 2 * EDGE, TILE), F32),
            pltpu.VMEM((images * (rows // TILE) + 1, cols + 2 * EDGE, TILE), F32),
            pltpu.VMEM((lanes, TILE, TILE), F32),
            pltpu.VMEM((lanes, TILE, TILE), F32),
            pltpu.VMEM((cols + 2 * EDGE, TILE), F32),
            pltpu.VMEM((cols + 2 * EDGE, TILE), F32),
            pltpu.VMEM((lanes, rows + 2 * EDGE, TILE), F32),
            pltpu.VMEM((lanes, rows + 2 * EDGE, TILE), F32),
            pltpu.VMEM((images, lanes + 2, ABOVE + rows + BELOW, TILE), BF16),
            pltpu.VMEM((images, 8, TILE), F32),
            pltpu.VMEM((images, 8, TILE), F32),
            pltpu.VMEM((tiles, TILE + ABOVE + BELOW, TILE), F32),
            pltpu.VMEM((cycles * tiles, 3 * TILE, TILE), BF16),
            pltpu.VMEM((images, rows, cols), BF16),
            pltpu.VMEM((rows, cols), BF16),
            pltpu.VMEM((2 * cycles + 1, rows // BOX, cols), F32),
            pltpu.VMEM((cycles + 1, rows // BOX, cols), F32),
            dma((channels, 3)),
            dma((images,)),
            dma((images, 2)),
            dma((images, 2)),
            dma((2,)),
            dma((2,)),
            dma((images, 2)),
            dma((images, 2)),
            dma((images,)),
            dma((images,)),
            dma((images, 3, 2)),
            dma((images, 3, 2)),
            dma((nx + sizes[0] // nx,)),
            dma((1,)),
        ],
        compiler_params=pltpu.CompilerParams(
            collective_id=0, has_side_effects=True, vmem_limit_bytes=56 * 1024 * 1024
        ),
    )(raw, flat, dark, shifts, fractions)
    return registered, scores


def solution(mesh):
    sizes = (mesh.shape["cyc"], mesh.shape["row"], mesh.shape["col"])
    return jax.shard_map(
        functools.partial(body, sizes),
        mesh=mesh,
        in_specs=(
            P("cyc", None, "row", "col"),
            P(None, "row", "col"),
            P(None, "row", "col"),
            P("cyc", "row", "col", None),
            P("cyc", "row", "col", None),
        ),
        out_specs=(P("cyc", None, "row", "col"), P("cyc", "row", "col")),
        check_vma=False,
    )
```

```python
import functools
import math

import jax
import jax.numpy as jnp
from jax import lax
from jax.experimental import pallas as pl
from jax.experimental.pallas import tpu as pltpu
from jax.sharding import PartitionSpec as P

TILE = 128
MARGIN = 8
ABOVE = 48
BELOW = 64
EDGE = 16
CHUNK = 136
BOX = 32
LAG = 2
MESH = pl.DeviceIdType.MESH
F32 = jnp.float32
BF16 = jnp.bfloat16


def spread_three(source, target, combine, start, count):
    for at in range(start, start + count, CHUNK):
        size = min(CHUNK, start + count - at)
        near = combine(source[pl.ds(at - 1, size), :], source[pl.ds(at, size), :])
        target[pl.ds(at, size), :] = combine(near, source[pl.ds(at + 1, size), :])


def spread_nine(source, combine, at, size):
    near = combine(source[pl.ds(at - 3, size), :], source[pl.ds(at, size), :])
    return combine(near, source[pl.ds(at + 3, size), :])


def kernel(
    sizes, raw, flat, dark, shifts_in, fractions_in, out, scores, shifts, fractions,
    rawv, flatv, darkv, corr, tall, brims, brims_back, wide1, wide2, three, back, hat, next_s, next_r, side_s, side_r, corner_s, corner_r, mixed, weights, reg, panel,
    sums, means,
    in_sem, scalar_sem, out_sem, p_send, p_recv, c_send, c_recv, r_send, r_recv, n_send, n_recv, h_send, h_recv, b_send, b_recv,
):
    n_cyc, n_row, n_col, nx = sizes
    ny = n_cyc // nx
    channels, rows, cols = flat.shape
    cycles = raw.shape[0]
    images = cycles * channels
    halves = rows // TILE
    lanes = cols // TILE
    cyc, row, col = lax.axis_index("cyc"), lax.axis_index("row"), lax.axis_index("col")
    yy, xx = cyc // nx, cyc % nx
    has_up, has_down = row > 0, row < n_row - 1
    has_left, has_right = col > 0, col < n_col - 1
    up, down = {"row": row - 1}, {"row": row + 1}
    left, right = {"col": col - 1}, {"col": col + 1}

    def in_copies(k):
        return (
            pltpu.make_async_copy(raw.at[:, k], rawv.at[:, k], in_sem.at[k, 0]),
            pltpu.make_async_copy(flat.at[k], flatv.at[k], in_sem.at[k, 1]),
            pltpu.make_async_copy(dark.at[k], darkv.at[k], in_sem.at[k, 2]),
        )

    for k in range(channels):
        for copy in in_copies(k):
            copy.start()

    scalars = (
        pltpu.make_async_copy(shifts_in, shifts, scalar_sem.at[0]),
        pltpu.make_async_copy(fractions_in, fractions, scalar_sem.at[1]),
    )
    for copy in scalars:
        copy.start()

    barrier = pltpu.get_barrier_semaphore()

    def greet(device):
        pl.semaphore_signal(barrier, inc=1, device_id=device, device_id_type=MESH)

    for there, device in ((has_up, up), (has_down, down), (has_left, left), (has_right, right)):
        pl.when(there)(functools.partial(greet, device))
    for k in range(1, nx):
        greet({"cyc": yy * nx + lax.rem(xx + k, nx)})
    for k in range(1, ny):
        pl.when(yy == 0)(functools.partial(greet, {"cyc": k * nx + xx}))
    pl.when(yy > 0)(functools.partial(greet, {"cyc": xx}))

    next_s[...] = jnp.zeros(next_s.shape, F32)

    @pl.when(jnp.logical_not(has_up))
    def _():
        corr[:, :, MARGIN:EDGE, :] = jnp.zeros((images, lanes, MARGIN, TILE), F32)
        hat[:, :, 0:ABOVE, :] = jnp.zeros((images, lanes + 2, ABOVE, TILE), BF16)

    @pl.when(jnp.logical_not(has_down))
    def _():
        corr[:, :, EDGE + rows : EDGE + rows + MARGIN, :] = jnp.zeros((images, lanes, MARGIN, TILE), F32)
        hat[:, :, ABOVE + rows :, :] = jnp.zeros((images, lanes + 2, BELOW, TILE), BF16)

    @pl.when(jnp.logical_not(has_left))
    def _():
        tall[:, :, MARGIN:EDGE, :] = jnp.zeros((channels, halves * cycles + 1, MARGIN, TILE), F32)
        side_r[:, 1] = jnp.zeros((images, TILE, TILE), BF16)
        corner_r[:, 1] = jnp.zeros((images, BELOW, TILE), BF16)

    @pl.when(jnp.logical_not(has_right))
    def _():
        tall[:, :, EDGE + cols : EDGE + cols + MARGIN, :] = jnp.zeros((channels, halves * cycles + 1, MARGIN, TILE), F32)
        side_r[:, 0] = jnp.zeros((images, TILE, TILE), BF16)
        corner_r[:, 0] = jnp.zeros((images, BELOW, TILE), BF16)

    def one(flag):
        return jnp.where(flag, 1, 0)

    expected = one(has_up) + one(has_down) + one(has_left) + one(has_right)
    expected += nx - 1 + jnp.where(yy == 0, ny - 1, 1)
    pl.semaphore_wait(barrier, expected)

    def remote(source, target, send, recv, device):
        return pltpu.make_async_remote_copy(
            src_ref=source, dst_ref=target, send_sem=send, recv_sem=recv, device_id=device, device_id_type=MESH
        )

    def edge_rows(i):
        return (
            (has_down, has_up, remote(
                corr.at[i, :, pl.ds(rows + MARGIN, MARGIN)], corr.at[i, :, pl.ds(MARGIN, MARGIN)],
                p_send.at[i, 0], p_recv.at[i, 0], down)),
            (has_up, has_down, remote(
                corr.at[i, :, pl.ds(EDGE, MARGIN)], corr.at[i, :, pl.ds(EDGE + rows, MARGIN)],
                p_send.at[i, 1], p_recv.at[i, 1], up)),
        )

    def start(moves):
        for sends, _, copy in moves:
            pl.when(sends)(copy.start)

    def received(moves):
        for _, receives, copy in moves:
            pl.when(receives)(copy.wait_recv)

    def sent(moves):
        for sends, _, copy in moves:
            pl.when(sends)(copy.wait_send)

    def correct(k, carry):
        for copy in in_copies(k):
            copy.wait()

        def block(b, carry):
            at = pl.ds(pl.multiple_of(b * 16, 16), 16)
            to = pl.ds(pl.multiple_of(b * 16 + EDGE, 16), 16)
            gain = 1.0 / flatv[k, at, :]
            offset = darkv[k, at, :]
            for c in range(cycles):
                value = (rawv[c, k, at, :].astype(F32) - offset) * gain
                for t in range(lanes):
                    corr[c * channels + k, t, to, :] = value[:, t * TILE : (t + 1) * TILE]
            return carry

        lax.fori_loop(0, rows // 16, block, 0)
        for c in range(cycles):
            start(edge_rows(c * channels + k))
        return carry

    lax.fori_loop(0, channels, correct, 0)

    tile_rows, tile_cols = rows // TILE, cols // TILE
    tiles = tile_rows * tile_cols
    source = lax.broadcasted_iota(jnp.int32, (3 * TILE, TILE), 0)
    target = lax.broadcasted_iota(jnp.int32, (3 * TILE, TILE), 1)
    apart = (source - target).astype(F32)

    def weigh(n, carry):
        c, rest = n // tiles, n % tiles
        i, j = rest // tile_cols, rest % tile_cols
        place = (shifts[c, i, 1, j] + TILE).astype(F32) + fractions[c, i, 1, j].astype(F32) / 8.0
        weights[n] = jnp.maximum(1.0 - jnp.abs(apart - place), 0.0).astype(BF16)
        return carry

    for copy in scalars:
        copy.wait()
    lax.fori_loop(0, cycles * tiles, weigh, 0)

    brims[:, cycles * MARGIN :, :] = jnp.zeros((lanes, TILE - cycles * MARGIN, TILE), F32)
    upper = lax.broadcasted_iota(jnp.int32, (MARGIN, TILE), 0) >= MARGIN // 2

    def edge_cols(k):
        return (
            (has_left, has_right, remote(
                tall.at[k, :, pl.ds(EDGE, MARGIN)], tall.at[k, :, pl.ds(EDGE + cols, MARGIN)],
                c_send.at[k, 0], c_recv.at[k, 0], left)),
            (has_right, has_left, remote(
                tall.at[k, :, pl.ds(cols + MARGIN, MARGIN)], tall.at[k, :, pl.ds(MARGIN, MARGIN)],
                c_send.at[k, 1], c_recv.at[k, 1], right)),
        )

    def erode(k):
        def one_cycle(c, carry):
            i = c * channels + k
            received(edge_rows(i))
            for t in range(lanes):
                spread_three(corr.at[i, t], three.at[t], jnp.minimum, MARGIN, rows + 2 * MARGIN)
            for t in range(lanes):
                for b in range(halves):
                    value = spread_nine(three.at[t], jnp.minimum, EDGE + b * TILE, TILE)
                    tall[k, halves * c + b, EDGE + t * TILE : EDGE + (t + 1) * TILE, :] = value.T
                above = spread_nine(three.at[t], jnp.minimum, MARGIN, MARGIN)
                below = spread_nine(three.at[t], jnp.minimum, EDGE + rows, MARGIN)
                brims[t, pl.ds(pl.multiple_of(MARGIN * c, MARGIN), MARGIN), :] = jnp.where(upper, above, below)
            return carry

        lax.fori_loop(0, cycles, one_cycle, 0)
        for t in range(lanes):
            tall[k, halves * cycles, EDGE + t * TILE : EDGE + (t + 1) * TILE, :] = brims[t].T
        start(edge_cols(k))

    def across(k, n, place):
        spread_three(tall.at[k, n], wide1, jnp.minimum, MARGIN, cols + 2 * MARGIN)
        for at in range(MARGIN, cols + EDGE + MARGIN, CHUNK):
            size = min(CHUNK, cols + EDGE + MARGIN - at)
            wide2[at : at + size, :] = spread_nine(wide1, jnp.minimum, at, size)
        spread_three(wide2, wide1, jnp.maximum, MARGIN, cols + 2 * MARGIN)
        for t in range(lanes):
            place(t, spread_nine(wide1, jnp.maximum, EDGE + t * TILE, TILE).T)

    def keep_brims(t, value):
        brims_back[t] = value

    def hat_rows(i):
        blocks = pl.ds(1, lanes)
        return (
            (has_down, has_up, remote(
                hat.at[i, blocks, pl.ds(rows, ABOVE)], hat.at[i, blocks, pl.ds(0, ABOVE)],
                r_send.at[i, 0], r_recv.at[i, 0], down)),
            (has_up, has_down, remote(
                hat.at[i, blocks, pl.ds(ABOVE, ABOVE)], hat.at[i, blocks, pl.ds(ABOVE + rows, ABOVE)],
                r_send.at[i, 1], r_recv.at[i, 1], up)),
            (has_up, has_down, remote(next_s.at[i], next_r.at[i], n_send.at[i], n_recv.at[i], up)),
        )

    def hat_cols(i, part):
        ours, theirs = ((side_s, side_r), (corner_s, corner_r))[part]
        return (
            (has_left, has_right, remote(
                ours.at[i, 0], theirs.at[i, 0], h_send.at[i, part, 0], h_recv.at[i, part, 0], left)),
            (has_right, has_left, remote(
                ours.at[i, 1], theirs.at[i, 1], h_send.at[i, part, 1], h_recv.at[i, part, 1], right)),
        )

    def packed(first, second, side):
        early = lax.broadcasted_iota(jnp.int32, first.shape, 1) < TILE // 2
        other = pltpu.roll(second, TILE // 2, 1)
        return (jnp.where(early, first, other) if side == 0 else jnp.where(early, other, first)).astype(BF16)

    def tophat(k, c):
        i = c * channels + k
        for b in range(halves):
            def keep(t, value, b=b):
                back[t, EDGE + b * TILE : EDGE + (b + 1) * TILE, :] = value

            across(k, halves * c + b, keep)
        for t in range(lanes):
            ends = brims_back[t, pl.ds(pl.multiple_of(MARGIN * c, MARGIN), MARGIN), :]
            back[t, MARGIN:EDGE, :] = ends
            back[t, EDGE + rows : EDGE + rows + MARGIN, :] = ends
        for t in range(lanes):
            spread_three(back.at[t], three.at[t], jnp.maximum, MARGIN, rows + 2 * MARGIN)
        for t in range(lanes):
            values = []
            for b in range(halves):
                opened = spread_nine(three.at[t], jnp.maximum, EDGE + b * TILE, TILE)
                values.append(corr[i, t, EDGE + b * TILE : EDGE + (b + 1) * TILE, :] - opened)
                hat[i, t + 1, ABOVE + b * TILE : ABOVE + (b + 1) * TILE, :] = values[b].astype(BF16)
            next_s[i, t : t + 1, :] = values[0][ABOVE : ABOVE + 1].astype(BF16).astype(F32)
            if t == 0:
                side_s[i, 0] = packed(values[0], values[1], 0)
            if t == lanes - 1:
                side_s[i, 1] = packed(values[0], values[1], 1)
        start(hat_rows(i))
        start(hat_cols(i, 0))

    def corners(i):
        received(hat_rows(i))

        @pl.when(has_down)
        def _():
            first = lax.broadcasted_iota(jnp.int32, (16, TILE), 0) == 0
            for t in range(lanes):
                value = jnp.where(first, next_r[i, t : t + 1, :], 0.0)
                hat[i, t + 1, ABOVE + rows + ABOVE :, :] = value.astype(BF16)

        for side, t in ((0, 1), (1, lanes)):
            above = hat[i, t, 0:BELOW, :].astype(F32)
            below = hat[i, t, ABOVE + rows :, :].astype(F32)
            corner_s[i, side] = packed(above, below, side)
        start(hat_cols(i, 1))

    def out_copy(i):
        return pltpu.make_async_copy(reg.at[i], out.at[i // channels, i % channels], out_sem.at[i])

    def resample(i):
        for part in range(2):
            received(hat_cols(i, part))
        for side, t in ((0, lanes + 1), (1, 0)):
            middle, ends = side_r[i, side], corner_r[i, side]
            hat[i, t, ABOVE : ABOVE + TILE, :] = middle
            hat[i, t, ABOVE + TILE : ABOVE + rows, :] = pltpu.roll(middle.astype(F32), TILE // 2, 1).astype(BF16)
            hat[i, t, 0:ABOVE, :] = ends[0:ABOVE]
            hat[i, t, ABOVE + rows :, :] = pltpu.roll(ends.astype(F32), TILE // 2, 1).astype(BF16)
        c = i // channels
        span = TILE + ABOVE + BELOW
        for n in range(tiles):
            ti, tj = n // tile_cols, n % tile_cols
            window = pl.ds(ti * TILE, span)
            near = jnp.concatenate([hat[i, tj + t, window, :] for t in range(3)], axis=1)
            moved = jnp.dot(near, weights[c * tiles + n], preferred_element_type=F32)
            mixed[n] = pltpu.roll(moved, (span - ABOVE) - shifts[c, ti, 0, tj], 0)
            lower = fractions[c, ti, 0, tj].astype(F32) / 8.0
            value = mixed[n, 0:TILE, :] * (1.0 - lower) + mixed[n, 1 : TILE + 1, :] * lower
            reg[i, ti * TILE : (ti + 1) * TILE, tj * TILE : (tj + 1) * TILE] = value.astype(BF16)
        out_copy(i).start()

    part = rows // nx

    def quarter(n):
        return pl.ds(pl.multiple_of(n * part, part), part)

    def panel_copy(n, device, slot, lands):
        at = panel.at[quarter(n)]
        return remote(at, at, b_send.at[slot], b_recv.at[lands], {"cyc": device})

    def first_sends(act):
        for k in range(1, nx):
            act(panel_copy(k, k, k, 0))

    def column_sends(act):
        for k in range(1, ny):
            act(panel_copy(xx, k * nx + xx, nx + k, 0))

    def row_sends(act):
        for k in range(1, nx):
            to = lax.rem(xx + k, nx)

            def send(k=k, to=to):
                act(panel_copy(xx, yy * nx + to, nx + ny + k, k))

            pl.when(yy * nx + to > 0)(send)

    def begin(copy):
        copy.start()

    def end(copy):
        copy.wait_send()

    def own_quarter_arrives():
        panel_copy(xx, 0, 0, 0).wait_recv()

    def both(act):
        def run(c, carry):
            act(c)
            return carry

        lax.fori_loop(0, cycles, run, 0)

    def step(s, carry):
        @pl.when(s < channels)
        def _():
            erode(s)

        @pl.when((s >= 1) & (s < 1 + channels))
        def _():
            received(edge_cols(s - 1))
            across(s - 1, halves * cycles, keep_brims)
            both(lambda c: tophat(s - 1, c))

        @pl.when(s >= LAG + 1)
        def _():
            both(lambda c: resample(c * channels + s - LAG - 1))

        @pl.when((s == LAG + 1) & (cyc == 0))
        def _():
            panel[...] = reg[0]
            first_sends(begin)
            column_sends(begin)
            row_sends(begin)

        @pl.when((s == LAG + 2) & (yy == 0) & (xx > 0))
        def _():
            own_quarter_arrives()
            column_sends(begin)
            row_sends(begin)

        @pl.when((s == LAG + 3) & (yy > 0))
        def _():
            own_quarter_arrives()
            row_sends(begin)

        @pl.when((s >= LAG) & (s < LAG + channels))
        def _():
            both(lambda c: corners(c * channels + s - LAG))

        return carry

    lax.fori_loop(0, channels + LAG + 1, step, 0)

    @pl.when(cyc > 0)
    def _():
        for k in range(1, nx):
            panel_copy(lax.rem(xx + nx - k, nx), 0, 0, k).wait_recv()

    box_rows, box_cols = rows // BOX, cols // BOX
    gather = (lax.broadcasted_iota(jnp.int32, (cols, box_cols), 0) // BOX
              == lax.broadcasted_iota(jnp.int32, (cols, box_cols), 1)).astype(F32)
    spread = (lax.broadcasted_iota(jnp.int32, (box_cols, cols), 1) // BOX
              == lax.broadcasted_iota(jnp.int32, (box_cols, cols), 0)).astype(F32)
    exact = functools.partial(jnp.dot, precision=lax.Precision.HIGHEST, preferred_element_type=F32)
    area = 1.0 / (BOX * BOX)

    def stains(b):
        at = pl.ds(b * BOX, BOX)
        return [reg[c * channels, at, :].astype(F32) for c in range(cycles)] + [panel[at, :].astype(F32)]

    for b in range(box_rows):
        for n, value in enumerate(stains(b)):
            sums[n, pl.ds(b, 1), :] = jnp.sum(value, axis=0, keepdims=True)
    for n in range(cycles + 1):
        means[n] = exact(exact(sums[n], gather) * area, spread)
    for b in range(box_rows):
        centred = [value - means[n, pl.ds(b, 1), :] for n, value in enumerate(stains(b))]
        fixed = centred[cycles]
        terms = [value * fixed for value in centred] + [value * value for value in centred[:cycles]]
        for n, value in enumerate(terms):
            sums[n, pl.ds(b, 1), :] = jnp.sum(value, axis=0, keepdims=True)
    fixed_var = exact(sums[cycles], gather) * area
    for c in range(cycles):
        covar = exact(sums[c], gather) * area
        var = exact(sums[cycles + 1 + c], gather) * area
        scores[c] = covar / jnp.sqrt(var * fixed_var + 1e-06)

    def finish(i, carry):
        sent(edge_rows(i))
        sent(hat_rows(i))
        for part in range(2):
            sent(hat_cols(i, part))
        out_copy(i).wait()
        return carry

    lax.fori_loop(0, images, finish, 0)
    for k in range(channels):
        sent(edge_cols(k))
    pl.when(cyc == 0)(functools.partial(first_sends, end))
    pl.when(yy == 0)(functools.partial(column_sends, end))
    row_sends(end)


def body(sizes, raw, flat, dark, shifts, fractions):
    shifts, fractions = jnp.swapaxes(shifts, 2, 3), jnp.swapaxes(fractions, 2, 3)
    cycles, channels, rows, cols = raw.shape
    images, lanes = cycles * channels, cols // TILE
    tiles = (rows // TILE) * lanes
    dma = pltpu.SemaphoreType.DMA
    anywhere = pl.BlockSpec(memory_space=pl.ANY)
    vmem = pl.BlockSpec(memory_space=pltpu.VMEM)
    nx = math.isqrt(sizes[0])
    registered, scores = pl.pallas_call(
        functools.partial(kernel, sizes + (nx,)),
        out_shape=(
            jax.ShapeDtypeStruct(raw.shape, BF16),
            jax.ShapeDtypeStruct((cycles, rows // BOX, cols // BOX), F32),
        ),
        in_specs=[anywhere] * 5,
        out_specs=(anywhere, vmem),
        scratch_shapes=[
            pltpu.SMEM(shifts.shape, jnp.int32),
            pltpu.SMEM(fractions.shape, jnp.int32),
            pltpu.VMEM(raw.shape, BF16),
            pltpu.VMEM(flat.shape, F32),
            pltpu.VMEM(dark.shape, F32),
            pltpu.VMEM((images, lanes, rows + 2 * EDGE, TILE), F32),
            pltpu.VMEM((channels, cycles * (rows // TILE) + 1, cols + 2 * EDGE, TILE), F32),
            pltpu.VMEM((lanes, TILE, TILE), F32),
            pltpu.VMEM((lanes, TILE, TILE), F32),
            pltpu.VMEM((cols + 2 * EDGE, TILE), F32),
            pltpu.VMEM((cols + 2 * EDGE, TILE), F32),
            pltpu.VMEM((lanes, rows + 2 * EDGE, TILE), F32),
            pltpu.VMEM((lanes, rows + 2 * EDGE, TILE), F32),
            pltpu.VMEM((images, lanes + 2, ABOVE + rows + BELOW, TILE), BF16),
            pltpu.VMEM((images, 8, TILE), F32),
            pltpu.VMEM((images, 8, TILE), F32),
            pltpu.VMEM((images, 2, TILE, TILE), BF16),
            pltpu.VMEM((images, 2, TILE, TILE), BF16),
            pltpu.VMEM((images, 2, BELOW, TILE), BF16),
            pltpu.VMEM((images, 2, BELOW, TILE), BF16),
            pltpu.VMEM((tiles, TILE + ABOVE + BELOW, TILE), F32),
            pltpu.VMEM((cycles * tiles, 3 * TILE, TILE), BF16),
            pltpu.VMEM((images, rows, cols), BF16),
            pltpu.VMEM((rows, cols), BF16),
            pltpu.VMEM((2 * cycles + 1, rows // BOX, cols), F32),
            pltpu.VMEM((cycles + 1, rows // BOX, cols), F32),
            dma((channels, 3)),
            dma((2,)),
            dma((images,)),
            dma((images, 2)),
            dma((images, 2)),
            dma((channels, 2)),
            dma((channels, 2)),
            dma((images, 2)),
            dma((images, 2)),
            dma((images,)),
            dma((images,)),
            dma((images, 2, 2)),
            dma((images, 2, 2)),
            dma((2 * nx + sizes[0] // nx,)),
            dma((nx,)),
        ],
        compiler_params=pltpu.CompilerParams(
            collective_id=0, has_side_effects=True, vmem_limit_bytes=56 * 1024 * 1024
        ),
    )(raw, flat, dark, shifts, fractions)
    return registered, scores


def solution(mesh):
    sizes = (mesh.shape["cyc"], mesh.shape["row"], mesh.shape["col"])
    return jax.shard_map(
        functools.partial(body, sizes),
        mesh=mesh,
        in_specs=(
            P("cyc", None, "row", "col"),
            P(None, "row", "col"),
            P(None, "row", "col"),
            P("cyc", "row", "col", None),
            P("cyc", "row", "col", None),
        ),
        out_specs=(P("cyc", None, "row", "col"), P("cyc", "row", "col")),
        check_vma=False,
    )
```

```python
import functools
import math

import jax
import jax.numpy as jnp
from jax import lax
from jax.experimental import pallas as pl
from jax.experimental.pallas import tpu as pltpu
from jax.sharding import PartitionSpec as P

TILE = 128
MARGIN = 8
ABOVE = 48
BELOW = 64
EDGE = 16
CHUNK = 136
BOX = 32
LAG = 2
MESH = pl.DeviceIdType.MESH
F32 = jnp.float32
BF16 = jnp.bfloat16


def spread_three(source, target, combine, start, count):
    for at in range(start, start + count, CHUNK):
        size = min(CHUNK, start + count - at)
        near = combine(source[pl.ds(at - 1, size), :], source[pl.ds(at, size), :])
        target[pl.ds(at, size), :] = combine(near, source[pl.ds(at + 1, size), :])


def spread_nine(source, combine, at, size):
    near = combine(source[pl.ds(at - 3, size), :], source[pl.ds(at, size), :])
    return combine(near, source[pl.ds(at + 3, size), :])


def kernel(
    sizes, raw, flat, dark, shifts_in, fractions_in, out, scores, shifts, fractions,
    rawv, flatv, darkv, corr, tall, brims, brims_back, wide1, wide2, three, back, hat, next_s, next_r, side_s, side_r, corner_s, corner_r, mixed, weights, reg, panel,
    sums, means,
    in_sem, scalar_sem, out_sem, p_send, p_recv, c_send, c_recv, r_send, r_recv, n_send, n_recv, h_send, h_recv, b_send, b_recv,
):
    n_cyc, n_row, n_col, nx = sizes
    ny = n_cyc // nx
    channels, rows, cols = flat.shape
    cycles = raw.shape[0]
    images = cycles * channels
    halves = rows // TILE
    lanes = cols // TILE
    cyc, row, col = lax.axis_index("cyc"), lax.axis_index("row"), lax.axis_index("col")
    yy, xx = cyc // nx, cyc % nx
    has_up, has_down = row > 0, row < n_row - 1
    has_left, has_right = col > 0, col < n_col - 1
    up, down = {"row": row - 1}, {"row": row + 1}
    left, right = {"col": col - 1}, {"col": col + 1}

    inner = pl.ds(16, rows - 32)

    def in_copies(k):
        return (
            pltpu.make_async_copy(raw.at[:, k, inner], rawv.at[:, k, inner], in_sem.at[k, 0]),
            pltpu.make_async_copy(flat.at[k, inner], flatv.at[k, inner], in_sem.at[k, 1]),
            pltpu.make_async_copy(dark.at[k, inner], darkv.at[k, inner], in_sem.at[k, 2]),
        )

    def edge_copies(n):
        at = pl.ds((0, rows - 16)[n], 16)
        return (
            pltpu.make_async_copy(raw.at[:, :, at], rawv.at[:, :, at], in_sem.at[channels + n, 0]),
            pltpu.make_async_copy(flat.at[:, at], flatv.at[:, at], in_sem.at[channels + n, 1]),
            pltpu.make_async_copy(dark.at[:, at], darkv.at[:, at], in_sem.at[channels + n, 2]),
        )

    for n in range(2):
        for copy in edge_copies(n):
            copy.start()
    for k in range(channels):
        for copy in in_copies(k):
            copy.start()

    scalars = (
        pltpu.make_async_copy(shifts_in, shifts, scalar_sem.at[0]),
        pltpu.make_async_copy(fractions_in, fractions, scalar_sem.at[1]),
    )
    for copy in scalars:
        copy.start()

    barrier = pltpu.get_barrier_semaphore()

    def greet(device):
        pl.semaphore_signal(barrier, inc=1, device_id=device, device_id_type=MESH)

    for there, device in ((has_up, up), (has_down, down), (has_left, left), (has_right, right)):
        pl.when(there)(functools.partial(greet, device))
    for k in range(1, nx):
        greet({"cyc": yy * nx + lax.rem(xx + k, nx)})
    for k in range(1, ny):
        pl.when(yy == 0)(functools.partial(greet, {"cyc": k * nx + xx}))
    pl.when(yy > 0)(functools.partial(greet, {"cyc": xx}))

    next_s[...] = jnp.zeros(next_s.shape, F32)

    @pl.when(jnp.logical_not(has_up))
    def _():
        corr[:, :, MARGIN:EDGE, :] = jnp.zeros((images, lanes, MARGIN, TILE), F32)
        hat[:, :, 0:ABOVE, :] = jnp.zeros((images, lanes + 2, ABOVE, TILE), BF16)

    @pl.when(jnp.logical_not(has_down))
    def _():
        corr[:, :, EDGE + rows : EDGE + rows + MARGIN, :] = jnp.zeros((images, lanes, MARGIN, TILE), F32)
        hat[:, :, ABOVE + rows :, :] = jnp.zeros((images, lanes + 2, BELOW, TILE), BF16)

    @pl.when(jnp.logical_not(has_left))
    def _():
        tall[:, :, MARGIN:EDGE, :] = jnp.zeros((channels, halves * cycles + 1, MARGIN, TILE), F32)
        side_r[:, 1] = jnp.zeros((images, TILE, TILE), BF16)
        corner_r[:, 1] = jnp.zeros((images, BELOW, TILE), BF16)

    @pl.when(jnp.logical_not(has_right))
    def _():
        tall[:, :, EDGE + cols : EDGE + cols + MARGIN, :] = jnp.zeros((channels, halves * cycles + 1, MARGIN, TILE), F32)
        side_r[:, 0] = jnp.zeros((images, TILE, TILE), BF16)
        corner_r[:, 0] = jnp.zeros((images, BELOW, TILE), BF16)

    def one(flag):
        return jnp.where(flag, 1, 0)

    expected = one(has_up) + one(has_down) + one(has_left) + one(has_right)
    expected += nx - 1 + jnp.where(yy == 0, ny - 1, 1)
    def remote(source, target, send, recv, device):
        return pltpu.make_async_remote_copy(
            src_ref=source, dst_ref=target, send_sem=send, recv_sem=recv, device_id=device, device_id_type=MESH
        )

    def edge_rows(i):
        return (
            (has_down, has_up, remote(
                corr.at[i, :, pl.ds(rows + MARGIN, MARGIN)], corr.at[i, :, pl.ds(MARGIN, MARGIN)],
                p_send.at[i, 0], p_recv.at[i, 0], down)),
            (has_up, has_down, remote(
                corr.at[i, :, pl.ds(EDGE, MARGIN)], corr.at[i, :, pl.ds(EDGE + rows, MARGIN)],
                p_send.at[i, 1], p_recv.at[i, 1], up)),
        )

    def start(moves):
        for sends, _, copy in moves:
            pl.when(sends)(copy.start)

    def received(moves):
        for _, receives, copy in moves:
            pl.when(receives)(copy.wait_recv)

    def sent(moves):
        for sends, _, copy in moves:
            pl.when(sends)(copy.wait_send)

    def correct(k, b):
        at = pl.ds(pl.multiple_of(b * 16, 16), 16)
        to = pl.ds(pl.multiple_of(b * 16 + EDGE, 16), 16)
        gain = 1.0 / flatv[k, at, :]
        offset = darkv[k, at, :]
        for c in range(cycles):
            value = (rawv[c, k, at, :].astype(F32) - offset) * gain
            for t in range(lanes):
                corr[c * channels + k, t, to, :] = value[:, t * TILE : (t + 1) * TILE]

    def correct_edges(k, carry):
        correct(k, 0)
        correct(k, rows // 16 - 1)
        return carry

    def send_edges(k, carry):
        for c in range(cycles):
            start(edge_rows(c * channels + k))
        return carry

    def correct_inner(k, carry):
        for copy in in_copies(k):
            copy.wait()

        def block(b, carry):
            correct(k, b)
            return carry

        lax.fori_loop(1, rows // 16 - 1, block, 0)
        return carry

    for n in range(2):
        for copy in edge_copies(n):
            copy.wait()
    lax.fori_loop(0, channels, correct_edges, 0)
    pl.semaphore_wait(barrier, expected)
    lax.fori_loop(0, channels, send_edges, 0)
    lax.fori_loop(0, channels, correct_inner, 0)

    tile_rows, tile_cols = rows // TILE, cols // TILE
    tiles = tile_rows * tile_cols
    source = lax.broadcasted_iota(jnp.int32, (3 * TILE, TILE), 0)
    target = lax.broadcasted_iota(jnp.int32, (3 * TILE, TILE), 1)
    apart = (source - target).astype(F32)

    def weigh(n, carry):
        c, rest = n // tiles, n % tiles
        i, j = rest // tile_cols, rest % tile_cols
        place = (shifts[c, i, 1, j] + TILE).astype(F32) + fractions[c, i, 1, j].astype(F32) / 8.0
        weights[n] = jnp.maximum(1.0 - jnp.abs(apart - place), 0.0).astype(BF16)
        return carry

    for copy in scalars:
        copy.wait()
    lax.fori_loop(0, cycles * tiles, weigh, 0)

    brims[:, cycles * MARGIN :, :] = jnp.zeros((lanes, TILE - cycles * MARGIN, TILE), F32)
    upper = lax.broadcasted_iota(jnp.int32, (MARGIN, TILE), 0) >= MARGIN // 2

    def edge_cols(k):
        return (
            (has_left, has_right, remote(
                tall.at[k, :, pl.ds(EDGE, MARGIN)], tall.at[k, :, pl.ds(EDGE + cols, MARGIN)],
                c_send.at[k, 0], c_recv.at[k, 0], left)),
            (has_right, has_left, remote(
                tall.at[k, :, pl.ds(cols + MARGIN, MARGIN)], tall.at[k, :, pl.ds(MARGIN, MARGIN)],
                c_send.at[k, 1], c_recv.at[k, 1], right)),
        )

    def erode(k):
        def one_cycle(c, carry):
            i = c * channels + k
            received(edge_rows(i))
            for t in range(lanes):
                spread_three(corr.at[i, t], three.at[t], jnp.minimum, MARGIN, rows + 2 * MARGIN)
            for t in range(lanes):
                for b in range(halves):
                    value = spread_nine(three.at[t], jnp.minimum, EDGE + b * TILE, TILE)
                    tall[k, halves * c + b, EDGE + t * TILE : EDGE + (t + 1) * TILE, :] = value.T
                above = spread_nine(three.at[t], jnp.minimum, MARGIN, MARGIN)
                below = spread_nine(three.at[t], jnp.minimum, EDGE + rows, MARGIN)
                brims[t, pl.ds(pl.multiple_of(MARGIN * c, MARGIN), MARGIN), :] = jnp.where(upper, above, below)
            return carry

        lax.fori_loop(0, cycles, one_cycle, 0)
        for t in range(lanes):
            tall[k, halves * cycles, EDGE + t * TILE : EDGE + (t + 1) * TILE, :] = brims[t].T
        start(edge_cols(k))

    def across(k, n, place):
        spread_three(tall.at[k, n], wide1, jnp.minimum, MARGIN, cols + 2 * MARGIN)
        for at in range(MARGIN, cols + EDGE + MARGIN, CHUNK):
            size = min(CHUNK, cols + EDGE + MARGIN - at)
            wide2[at : at + size, :] = spread_nine(wide1, jnp.minimum, at, size)
        spread_three(wide2, wide1, jnp.maximum, MARGIN, cols + 2 * MARGIN)
        for t in range(lanes):
            place(t, spread_nine(wide1, jnp.maximum, EDGE + t * TILE, TILE).T)

    def keep_brims(t, value):
        brims_back[t] = value

    def hat_rows(i):
        blocks = pl.ds(1, lanes)
        return (
            (has_down, has_up, remote(
                hat.at[i, blocks, pl.ds(rows, ABOVE)], hat.at[i, blocks, pl.ds(0, ABOVE)],
                r_send.at[i, 0], r_recv.at[i, 0], down)),
            (has_up, has_down, remote(
                hat.at[i, blocks, pl.ds(ABOVE, ABOVE)], hat.at[i, blocks, pl.ds(ABOVE + rows, ABOVE)],
                r_send.at[i, 1], r_recv.at[i, 1], up)),
            (has_up, has_down, remote(next_s.at[i], next_r.at[i], n_send.at[i], n_recv.at[i], up)),
        )

    def hat_cols(i, part):
        ours, theirs = ((side_s, side_r), (corner_s, corner_r))[part]
        return (
            (has_left, has_right, remote(
                ours.at[i, 0], theirs.at[i, 0], h_send.at[i, part, 0], h_recv.at[i, part, 0], left)),
            (has_right, has_left, remote(
                ours.at[i, 1], theirs.at[i, 1], h_send.at[i, part, 1], h_recv.at[i, part, 1], right)),
        )

    def packed(first, second, side):
        early = lax.broadcasted_iota(jnp.int32, first.shape, 1) < TILE // 2
        other = pltpu.roll(second, TILE // 2, 1)
        return (jnp.where(early, first, other) if side == 0 else jnp.where(early, other, first)).astype(BF16)

    def tophat(k, c):
        i = c * channels + k
        for b in range(halves):
            def keep(t, value, b=b):
                back[t, EDGE + b * TILE : EDGE + (b + 1) * TILE, :] = value

            across(k, halves * c + b, keep)
        for t in range(lanes):
            ends = brims_back[t, pl.ds(pl.multiple_of(MARGIN * c, MARGIN), MARGIN), :]
            back[t, MARGIN:EDGE, :] = ends
            back[t, EDGE + rows : EDGE + rows + MARGIN, :] = ends
        for t in range(lanes):
            spread_three(back.at[t], three.at[t], jnp.maximum, MARGIN, rows + 2 * MARGIN)
        for t in range(lanes):
            values = []
            for b in range(halves):
                opened = spread_nine(three.at[t], jnp.maximum, EDGE + b * TILE, TILE)
                values.append(corr[i, t, EDGE + b * TILE : EDGE + (b + 1) * TILE, :] - opened)
                hat[i, t + 1, ABOVE + b * TILE : ABOVE + (b + 1) * TILE, :] = values[b].astype(BF16)
            next_s[i, t : t + 1, :] = values[0][ABOVE : ABOVE + 1].astype(BF16).astype(F32)
            if t == 0:
                side_s[i, 0] = packed(values[0], values[1], 0)
            if t == lanes - 1:
                side_s[i, 1] = packed(values[0], values[1], 1)
        start(hat_rows(i))
        start(hat_cols(i, 0))

    def corners(i):
        received(hat_rows(i))

        @pl.when(has_down)
        def _():
            first = lax.broadcasted_iota(jnp.int32, (16, TILE), 0) == 0
            for t in range(lanes):
                value = jnp.where(first, next_r[i, t : t + 1, :], 0.0)
                hat[i, t + 1, ABOVE + rows + ABOVE :, :] = value.astype(BF16)

        for side, t in ((0, 1), (1, lanes)):
            above = hat[i, t, 0:BELOW, :].astype(F32)
            below = hat[i, t, ABOVE + rows :, :].astype(F32)
            corner_s[i, side] = packed(above, below, side)
        start(hat_cols(i, 1))

    def out_copy(i):
        return pltpu.make_async_copy(reg.at[i], out.at[i // channels, i % channels], out_sem.at[i])

    def blend(i, columns):
        c = i // channels
        span = TILE + ABOVE + BELOW
        for n in range(tiles):
            ti, tj = n // tile_cols, n % tile_cols
            if tj not in columns:
                continue
            window = pl.ds(ti * TILE, span)
            near = jnp.concatenate([hat[i, tj + t, window, :] for t in range(3)], axis=1)
            moved = jnp.dot(near, weights[c * tiles + n], preferred_element_type=F32)
            mixed[n] = pltpu.roll(moved, (span - ABOVE) - shifts[c, ti, 0, tj], 0)
            lower = fractions[c, ti, 0, tj].astype(F32) / 8.0
            value = mixed[n, 0:TILE, :] * (1.0 - lower) + mixed[n, 1 : TILE + 1, :] * lower
            reg[i, ti * TILE : (ti + 1) * TILE, tj * TILE : (tj + 1) * TILE] = value.astype(BF16)

    def resample(i):
        for part in range(2):
            received(hat_cols(i, part))
        for side, t in ((0, lanes + 1), (1, 0)):
            middle, ends = side_r[i, side], corner_r[i, side]
            hat[i, t, ABOVE : ABOVE + TILE, :] = middle
            hat[i, t, ABOVE + TILE : ABOVE + rows, :] = pltpu.roll(middle.astype(F32), TILE // 2, 1).astype(BF16)
            hat[i, t, 0:ABOVE, :] = ends[0:ABOVE]
            hat[i, t, ABOVE + rows :, :] = pltpu.roll(ends.astype(F32), TILE // 2, 1).astype(BF16)
        blend(i, (0, tile_cols - 1))
        out_copy(i).start()

    part = rows // nx

    def quarter(n):
        return pl.ds(pl.multiple_of(n * part, part), part)

    def panel_copy(n, device, slot, lands):
        at = panel.at[quarter(n)]
        return remote(at, at, b_send.at[slot], b_recv.at[lands], {"cyc": device})

    def first_sends(act):
        for k in range(1, nx):
            act(panel_copy(k, k, k, 0))

    def column_sends(act):
        for k in range(1, ny):
            act(panel_copy(xx, k * nx + xx, nx + k, 0))

    def row_sends(act):
        for k in range(1, nx):
            to = lax.rem(xx + k, nx)

            def send(k=k, to=to):
                act(panel_copy(xx, yy * nx + to, nx + ny + k, k))

            pl.when(yy * nx + to > 0)(send)

    def begin(copy):
        copy.start()

    def end(copy):
        copy.wait_send()

    def own_quarter_arrives():
        panel_copy(xx, 0, 0, 0).wait_recv()

    def both(act):
        def run(c, carry):
            act(c)
            return carry

        lax.fori_loop(0, cycles, run, 0)

    def correlate():
        @pl.when(cyc > 0)
        def _():
            for k in range(1, nx):
                panel_copy(lax.rem(xx + nx - k, nx), 0, 0, k).wait_recv()

        box_rows, box_cols = rows // BOX, cols // BOX
        gather = (lax.broadcasted_iota(jnp.int32, (cols, box_cols), 0) // BOX
                  == lax.broadcasted_iota(jnp.int32, (cols, box_cols), 1)).astype(F32)
        spread = (lax.broadcasted_iota(jnp.int32, (box_cols, cols), 1) // BOX
                  == lax.broadcasted_iota(jnp.int32, (box_cols, cols), 0)).astype(F32)
        exact = functools.partial(jnp.dot, precision=lax.Precision.HIGHEST, preferred_element_type=F32)
        area = 1.0 / (BOX * BOX)

        def stains(b):
            at = pl.ds(b * BOX, BOX)
            return [reg[c * channels, at, :].astype(F32) for c in range(cycles)] + [panel[at, :].astype(F32)]

        for b in range(box_rows):
            for n, value in enumerate(stains(b)):
                sums[n, pl.ds(b, 1), :] = jnp.sum(value, axis=0, keepdims=True)
        for n in range(cycles + 1):
            means[n] = exact(exact(sums[n], gather) * area, spread)
        for b in range(box_rows):
            centred = [value - means[n, pl.ds(b, 1), :] for n, value in enumerate(stains(b))]
            fixed = centred[cycles]
            terms = [value * fixed for value in centred] + [value * value for value in centred[:cycles]]
            for n, value in enumerate(terms):
                sums[n, pl.ds(b, 1), :] = jnp.sum(value, axis=0, keepdims=True)
        fixed_var = exact(sums[cycles], gather) * area
        for c in range(cycles):
            covar = exact(sums[c], gather) * area
            var = exact(sums[cycles + 1 + c], gather) * area
            scores[c] = covar / jnp.sqrt(var * fixed_var + 1e-06)

    def step(s, carry):
        @pl.when(s < channels)
        def _():
            erode(s)

        @pl.when((s >= 1) & (s < 1 + channels))
        def _():
            received(edge_cols(s - 1))
            across(s - 1, halves * cycles, keep_brims)
            both(lambda c: tophat(s - 1, c))

        @pl.when((s == LAG + 2) & (yy == 0) & (xx > 0))
        def _():
            own_quarter_arrives()
            column_sends(begin)
            row_sends(begin)

        @pl.when((s == LAG + 3) & (yy > 0))
        def _():
            own_quarter_arrives()
            row_sends(begin)

        @pl.when(s >= LAG + 1)
        def _():
            resample(s - LAG - 1)

        @pl.when((s == LAG + 1) & (cyc == 0))
        def _():
            panel[...] = reg[0]
            first_sends(begin)
            column_sends(begin)
            row_sends(begin)

        @pl.when(s >= LAG + 1)
        def _():
            def run(c, carry):
                resample(c * channels + s - LAG - 1)
                return carry

            lax.fori_loop(1, cycles, run, 0)

        pl.when(s == LAG + channels)(correlate)

        @pl.when((s >= LAG) & (s < LAG + channels))
        def _():
            both(lambda c: corners(c * channels + s - LAG))
            both(lambda c: blend(c * channels + s - LAG, range(1, tile_cols - 1)))

        return carry

    lax.fori_loop(0, channels + LAG + 1, step, 0)

    def finish(i, carry):
        sent(edge_rows(i))
        sent(hat_rows(i))
        for part in range(2):
            sent(hat_cols(i, part))
        out_copy(i).wait()
        return carry

    lax.fori_loop(0, images, finish, 0)
    for k in range(channels):
        sent(edge_cols(k))
    pl.when(cyc == 0)(functools.partial(first_sends, end))
    pl.when(yy == 0)(functools.partial(column_sends, end))
    row_sends(end)


def body(sizes, raw, flat, dark, shifts, fractions):
    shifts, fractions = jnp.swapaxes(shifts, 2, 3), jnp.swapaxes(fractions, 2, 3)
    cycles, channels, rows, cols = raw.shape
    images, lanes = cycles * channels, cols // TILE
    tiles = (rows // TILE) * lanes
    dma = pltpu.SemaphoreType.DMA
    anywhere = pl.BlockSpec(memory_space=pl.ANY)
    vmem = pl.BlockSpec(memory_space=pltpu.VMEM)
    nx = math.isqrt(sizes[0])
    registered, scores = pl.pallas_call(
        functools.partial(kernel, sizes + (nx,)),
        out_shape=(
            jax.ShapeDtypeStruct(raw.shape, BF16),
            jax.ShapeDtypeStruct((cycles, rows // BOX, cols // BOX), F32),
        ),
        in_specs=[anywhere] * 5,
        out_specs=(anywhere, vmem),
        scratch_shapes=[
            pltpu.SMEM(shifts.shape, jnp.int32),
            pltpu.SMEM(fractions.shape, jnp.int32),
            pltpu.VMEM(raw.shape, BF16),
            pltpu.VMEM(flat.shape, F32),
            pltpu.VMEM(dark.shape, F32),
            pltpu.VMEM((images, lanes, rows + 2 * EDGE, TILE), F32),
            pltpu.VMEM((channels, cycles * (rows // TILE) + 1, cols + 2 * EDGE, TILE), F32),
            pltpu.VMEM((lanes, TILE, TILE), F32),
            pltpu.VMEM((lanes, TILE, TILE), F32),
            pltpu.VMEM((cols + 2 * EDGE, TILE), F32),
            pltpu.VMEM((cols + 2 * EDGE, TILE), F32),
            pltpu.VMEM((lanes, rows + 2 * EDGE, TILE), F32),
            pltpu.VMEM((lanes, rows + 2 * EDGE, TILE), F32),
            pltpu.VMEM((images, lanes + 2, ABOVE + rows + BELOW, TILE), BF16),
            pltpu.VMEM((images, 8, TILE), F32),
            pltpu.VMEM((images, 8, TILE), F32),
            pltpu.VMEM((images, 2, TILE, TILE), BF16),
            pltpu.VMEM((images, 2, TILE, TILE), BF16),
            pltpu.VMEM((images, 2, BELOW, TILE), BF16),
            pltpu.VMEM((images, 2, BELOW, TILE), BF16),
            pltpu.VMEM((tiles, TILE + ABOVE + BELOW, TILE), F32),
            pltpu.VMEM((cycles * tiles, 3 * TILE, TILE), BF16),
            pltpu.VMEM((images, rows, cols), BF16),
            pltpu.VMEM((rows, cols), BF16),
            pltpu.VMEM((2 * cycles + 1, rows // BOX, cols), F32),
            pltpu.VMEM((cycles + 1, rows // BOX, cols), F32),
            dma((channels + 2, 3)),
            dma((2,)),
            dma((images,)),
            dma((images, 2)),
            dma((images, 2)),
            dma((channels, 2)),
            dma((channels, 2)),
            dma((images, 2)),
            dma((images, 2)),
            dma((images,)),
            dma((images,)),
            dma((images, 2, 2)),
            dma((images, 2, 2)),
            dma((2 * nx + sizes[0] // nx,)),
            dma((nx,)),
        ],
        compiler_params=pltpu.CompilerParams(
            collective_id=0, has_side_effects=True, vmem_limit_bytes=56 * 1024 * 1024
        ),
    )(raw, flat, dark, shifts, fractions)
    return registered, scores


def solution(mesh):
    sizes = (mesh.shape["cyc"], mesh.shape["row"], mesh.shape["col"])
    return jax.shard_map(
        functools.partial(body, sizes),
        mesh=mesh,
        in_specs=(
            P("cyc", None, "row", "col"),
            P(None, "row", "col"),
            P(None, "row", "col"),
            P("cyc", "row", "col", None),
            P("cyc", "row", "col", None),
        ),
        out_specs=(P("cyc", None, "row", "col"), P("cyc", "row", "col")),
        check_vma=False,
    )
```
